32 devices in a mesh: leaf: 4 (over y, x), row: 8 (over z, core).
Axes of the slice: x: 2, y: 2, z: 4, core: 2. Of those that a mesh axis runs over, the one named last changes fastest.
Arguments:
- sigma_root: float32 [2048, 2048], P(None, 'row')
- linv_one: bfloat16 [4, 2048, 2048], P('leaf', None, 'row'), as said below
- panel_one: bfloat16 [4, 512, 2048], P('leaf', None, 'row'), may hold values from -1.25 to 1.25
- tiles_one: int32 [4, 4], replicated, may hold values from 0 to 15, as said below
- mask_one: int32 [4, 4, 16], P('leaf', None, 'row'), may hold values 0 or 1
- linv_two: bfloat16 [4, 2048, 2048], P('leaf', None, 'row'), as said below
- panel_two: bfloat16 [4, 512, 2048], P('leaf', None, 'row'), may hold values from -1.25 to 1.25
- tiles_two: int32 [4, 4], replicated, may hold values from 0 to 15, as said below
- mask_two: int32 [4, 4, 16], P('leaf', None, 'row'), may hold values 0 or 1
- parent: int32 [4], replicated, may hold values from 0 to 3
Outputs:
- sigma_one: float32 [4, 2048, 2048], P('leaf', None, 'row')
- cross_one: float32 [4, 512, 2048], P('leaf', None, 'row')
- sigma_two: float32 [4, 2048, 2048], P('leaf', None, 'row')
- cross_two: float32 [4, 512, 2048], P('leaf', None, 'row')
The draws below stay inside these ranges and needn't reach their ends.
Inputs may be any that keep to these rules, and one draw needn't show every extreme that they name: `tiles_one`: each row holds 4 different tile numbers in increasing order. `tiles_two`: each row holds 4 different tile numbers in increasing order. `linv_one`: each block is lower triangular with a positive diagonal. `sigma_root`: symmetric. `linv_two`: each block is lower triangular with a positive diagonal.
All inputs are finite; a program needn't handle non-finite values. No bound on the sum of `mask_one` or of `mask_two` on one device may be relied on, other than what follows from the above.
Results may differ from the reference program's by a relative error of at most 0.00045.
Values may be sent and summed in bfloat16 or wider, within the bound.
A program may use at most 64 MiB of HBM per device.

```python
import math
import jax
import jax.numpy as jnp
from jax import lax

NS = 2048
TILE = 128
K = 4
P_SIZE = 4
NT = 16
KB = 512
N_LEAF = 4


def lower_inverse(key):
    key_noise, key_diag = jax.random.split(key)
    noise = jax.random.normal(key_noise, (NS, NS), jnp.float32) * (1.0 / math.sqrt(NS))
    index = jnp.arange(NS, dtype=jnp.int32)
    below = (index[:, None] > index[None, :]).astype(jnp.float32)
    diagonal = jax.random.uniform(key_diag, (NS,), jnp.float32, 0.6, 1.6)
    return (noise * below + jnp.diag(diagonal)).astype(jnp.bfloat16)


def tile_lists(key):
    row_keys = jax.random.split(key, P_SIZE)

    def one_row(row_key):
        return jnp.sort(jax.random.permutation(row_key, NT)[:K])
    return jax.vmap(one_row)(row_keys).astype(jnp.int32)


def draw_sigma_root(key, part):
    key_noise, key_diag = jax.random.split(jax.random.fold_in(key, 3), 2)
    noise = jax.random.normal(key_noise, (NS, NS), jnp.float32)
    symmetric = (noise + noise.T) * (0.35 / math.sqrt(NS))
    diagonal = jnp.exp(jax.random.uniform(key_diag, (NS,), jnp.float32, math.log(1.5), math.log(3.0)))
    result = symmetric + jnp.diag(diagonal)
    return result


def draw_linv_one(key, part):
    row_keys = jax.random.split(jax.random.fold_in(key, 5), P_SIZE)
    return jax.vmap(lower_inverse)(row_keys)


def draw_linv_two(key, part):
    row_keys = jax.random.split(jax.random.fold_in(key, 7), P_SIZE)
    return jax.vmap(lower_inverse)(row_keys)


def draw_tiles_one(key, part):
    return tile_lists(jax.random.fold_in(key, 11))


def draw_tiles_two(key, part):
    return tile_lists(jax.random.fold_in(key, 13))


def place_ends(values, stream_key, smallest, largest):
    place = [jax.random.randint(jax.random.fold_in(stream_key, axis), (), 0, length) for axis, length in enumerate(values.shape)]
    longest = values.shape.index(max(values.shape))
    neighbour = place[:longest] + [(place[longest] + 1) % values.shape[longest]] + place[longest + 1:]
    return values.at[tuple(place)].set(smallest).at[tuple(neighbour)].set(largest)


def steps_of(own_key, dims, shards, smallest, largest):
    factor_of = 1.0
    for dim, shards_of in shards:
        steps = jax.random.uniform(jax.random.fold_in(jax.random.fold_in(own_key, 6), dim), (shards_of,), jnp.float32, smallest / len(shards), largest / len(shards))
        factor_of = factor_of * jnp.repeat(jnp.exp(steps), dims[dim] // shards_of).reshape((-1,) + (1,) * (len(dims) - 1 - dim))
    return factor_of


def scatter_about(own_key, shape, spread, reach, shards=(), kind=jnp.bfloat16):
    values = jax.random.normal(own_key, shape, jnp.float32) * spread
    if len(shards) > 0:
        values = steps_of(own_key, shape, shards, -0.22, 0.18) * values
    return jnp.clip(values, min=-reach, max=reach).astype(kind)


def setup_inputs(seed: int = 0) -> dict:
    seeds = jax.random.split(jax.random.key(seed), 11)
    return {
        "sigma_root": draw_sigma_root(jax.random.fold_in(seeds[10], 71), 0),
        "linv_one": draw_linv_one(jax.random.fold_in(seeds[10], 71), 0),
        "panel_one": scatter_about(seeds[2], (P_SIZE, KB, NS), (2.0 / (K * TILE) ** 0.5), 1.25, ((0, 4), (2, 8))),
        "tiles_one": draw_tiles_one(jax.random.fold_in(seeds[10], 71), 0),
        "mask_one": place_ends((jax.random.randint(seeds[4], (P_SIZE, K, NT), 0, 4) < 3).astype(jnp.int32), jax.random.fold_in(seeds[4], 1), 0, 1),
        "linv_two": draw_linv_two(jax.random.fold_in(seeds[10], 71), 0),
        "panel_two": scatter_about(seeds[6], (P_SIZE, KB, NS), (2.0 / (K * TILE) ** 0.5), 1.25, ((0, 4), (2, 8))),
        "tiles_two": draw_tiles_two(jax.random.fold_in(seeds[10], 71), 0),
        "mask_two": place_ends((jax.random.randint(seeds[8], (P_SIZE, K, NT), 0, 4) < 3).astype(jnp.int32), jax.random.fold_in(seeds[8], 1), 0, 1),
        "parent": place_ends(jax.random.randint(seeds[9], (P_SIZE,), 0, N_LEAF), jax.random.fold_in(seeds[9], 1), 0, N_LEAF - 1).astype(jnp.int32),
    }


def pattern_rows(tile_list):
    offsets = jnp.arange(TILE, dtype=jnp.int32)
    return (tile_list[:, None].astype(jnp.int32) * TILE + offsets[None, :]).reshape(-1)


def expand_mask(tile_mask):
    return jnp.repeat(jnp.repeat(tile_mask, TILE, axis=0), TILE, axis=1)


def solve_block(ancestor, linv, panel, tile_list, tile_mask):
    row_list = pattern_rows(tile_list)
    select = jnp.take(jnp.take(ancestor, row_list, axis=0), row_list, axis=1)
    masked = panel * expand_mask(tile_mask).astype(jnp.bfloat16)
    upper_part = jnp.dot(masked, linv, preferred_element_type=jnp.float32)
    cross = -jnp.dot(select, upper_part, precision=lax.Precision.HIGHEST)
    linv_wide = linv.astype(jnp.float32)
    middle = linv_wide - jnp.dot(masked.astype(jnp.float32).T, cross, precision=lax.Precision.HIGHEST)
    sigma = jnp.dot(linv_wide.T, middle, precision=lax.Precision.HIGHEST)
    return sigma, cross


def reference(sigma_root, linv_one, panel_one, tiles_one, mask_one, linv_two, panel_two, tiles_two, mask_two, parent):
    def first_level(items):
        return solve_block(sigma_root, items[0], items[1], items[2], items[3])

    sigma_one, cross_one = lax.map(first_level, (linv_one, panel_one, tiles_one, mask_one))

    def second_level(items):
        ancestor = lax.dynamic_index_in_dim(sigma_one, items[4], 0, keepdims=False)
        return solve_block(ancestor, items[0], items[1], items[2], items[3])

    sigma_two, cross_two = lax.map(second_level, (linv_two, panel_two, tiles_two, mask_two, parent))
    return sigma_one, cross_one, sigma_two, cross_two
```

```python
import functools

import jax
import jax.numpy as jnp
from jax import lax
from jax.experimental import pallas as pl
from jax.experimental.pallas import tpu as pltpu
from jax.sharding import PartitionSpec as P

TILE = 128
MESH = pl.DeviceIdType.MESH
HIGH = lax.Precision.HIGH


def pattern_rows(tile_list):
    offsets = jnp.arange(TILE, dtype=jnp.int32)
    return (tile_list[..., None] * TILE + offsets).reshape(tile_list.shape[:-1] + (-1,))


def expand_mask(tile_mask):
    return jnp.repeat(jnp.repeat(tile_mask, TILE, axis=0), TILE, axis=1)


def gather_kernel(chips, panel_ref, linv_ref, whole_panel, *rest):
    blocks = rest[:chips]
    zrecv, zright, zleft, srecv, ssend, local = rest[chips:]
    width = panel_ref.shape[1]
    step = 2 * width
    row = lax.axis_index("row")
    z = lax.div(row, 2)
    core = lax.rem(row, 2)
    right, left, sibling = row + 2, row - 2, row + 1 - 2 * core

    barrier = pltpu.get_barrier_semaphore()

    def greet(device):
        pl.semaphore_signal(barrier, inc=1, device_id={"row": device}, device_id_type=MESH)

    greet(sibling)

    @pl.when(z > 0)
    def _():
        greet(left)

    @pl.when(z < chips - 1)
    def _():
        greet(right)

    @pl.when(jnp.logical_or(z == 0, z == chips - 1))
    def _():
        pl.semaphore_wait(barrier, 2)

    @pl.when(jnp.logical_and(z > 0, z < chips - 1))
    def _():
        pl.semaphore_wait(barrier, 3)

    def place(s, c, piece):
        if piece == 0:
            return whole_panel.at[:, pl.ds(pl.multiple_of((2 * s + c) * width, width), width)]
        return blocks[s].at[pl.ds((piece - 1) * step, step), pl.ds(pl.multiple_of(c * width, width), width)]

    def origin(s, piece):
        if piece == 0:
            return panel_ref
        return linv_ref.at[pl.ds((s + piece - 1) * step, step), :]

    def send(source, s, piece, sends, recvs, device):
        return pltpu.make_async_remote_copy(
            src_ref=source,
            dst_ref=place(s, core, piece),
            send_sem=sends.at[s, piece],
            recv_sem=recvs.at[s, piece],
            device_id={"row": device},
            device_id_type=MESH,
        )

    def pieces(s):
        return range(1 + chips - s)

    def copies(source, s, piece, go_right, go_left):
        out = []
        if go_right:
            out.append(send(source, s, piece, zright, zrecv, right))
        if go_left:
            out.append(send(source, s, piece, zleft, zrecv, left))
        out.append(send(source, s, piece, ssend, srecv, sibling))
        return out

    def own(s, piece):
        here = pltpu.make_async_copy(origin(s, piece), place(s, core, piece), local.at[piece])
        return copies(origin(s, piece), s, piece, s < chips - 1, s > 0) + [here]

    for s in range(chips):
        @pl.when(z == s)
        def _(s=s):
            for piece in pieces(s):
                for copy in own(s, piece):
                    copy.start()

    def routes(hops):
        for s in range(chips):
            if s + hops < chips:
                yield s, s + hops, s + hops < chips - 1, False
            if s - hops >= 0:
                yield s, s - hops, False, s - hops > 0

    def arrived(s, piece, recvs, c):
        pltpu.make_async_copy(place(s, c, piece), place(s, c, piece), recvs.at[s, piece]).wait()

    for hops in range(1, chips):
        for piece in range(chips + 1):
            for s, here, go_right, go_left in routes(hops):
                if piece in pieces(s):
                    @pl.when(z == here)
                    def _(s=s, piece=piece, go_right=go_right, go_left=go_left):
                        arrived(s, piece, zrecv, core)
                        for copy in copies(place(s, core, piece), s, piece, go_right, go_left):
                            copy.start()

    for s in range(chips):
        for piece in pieces(s):
            arrived(s, piece, srecv, 1 - core)

        @pl.when(z == s)
        def _(s=s):
            for piece in pieces(s):
                moves = own(s, piece)
                for copy in moves[:-1]:
                    copy.wait_send()
                moves[-1].wait()

    for hops in range(1, chips):
        for s, here, go_right, go_left in routes(hops):
            @pl.when(z == here)
            def _(s=s, go_right=go_right, go_left=go_left):
                for piece in pieces(s):
                    for copy in copies(place(s, core, piece), s, piece, go_right, go_left):
                        copy.wait_send()


def gather_block(panel, linv, chips, number):
    order, width = linv.shape
    rows = panel.shape[0]
    step = 2 * width
    kind = linv.dtype
    any_space = pl.BlockSpec(memory_space=pl.ANY)
    shapes = [jax.ShapeDtypeStruct((rows, order), kind)]
    shapes += [jax.ShapeDtypeStruct((order - s * step, step), kind) for s in range(chips)]
    moved = (rows * order + order * order) * 2
    out = pl.pallas_call(
        functools.partial(gather_kernel, chips),
        out_shape=shapes,
        in_specs=[any_space, any_space],
        out_specs=[any_space] * len(shapes),
        scratch_shapes=[pltpu.SemaphoreType.DMA((chips, chips + 1))] * 5
        + [pltpu.SemaphoreType.DMA((chips + 1,))],
        compiler_params=pltpu.CompilerParams(collective_id=number, has_side_effects=True),
        cost_estimate=pl.CostEstimate(flops=0, bytes_accessed=moved * 20, transcendentals=0),
        name="gather_%d" % number,
    )(panel, linv)
    return out[0], out[1:]


def spread_tiles(selected, tile_list):
    width = selected.shape[1]
    per = width // TILE
    row = lax.axis_index("row")
    parts = []
    for a in range(tile_list.shape[0]):
        tile = tile_list[a]
        piece = jnp.zeros((selected.shape[0], TILE), selected.dtype)
        for k in range(per):
            hit = tile == row * per + k
            piece = piece + jnp.where(hit, selected[:, k * TILE:(k + 1) * TILE], 0.0)
        parts.append(piece)
    return jnp.concatenate(parts, axis=1)


def finish_block(select, whole_panel, blocks, linv):
    width = linv.shape[1]
    step = 2 * width
    row = lax.axis_index("row")
    upper = jnp.concatenate(
        [
            jnp.dot(whole_panel[:, s * step:], block, preferred_element_type=jnp.float32)
            for s, block in enumerate(blocks)
        ],
        axis=1,
    )
    own = lax.dynamic_slice_in_dim(upper, row * width, width, 1)
    cross = -jnp.dot(select, own, precision=HIGH)
    gram = jnp.concatenate(
        [
            lax.dot_general(
                block, linv[s * step:], (((0,), (0,)), ((), ())), preferred_element_type=jnp.float32
            )
            for s, block in enumerate(blocks)
        ],
        axis=0,
    )
    sigma = gram - lax.dot_general(upper, cross, (((0,), (0,)), ((), ())), precision=HIGH)
    return sigma, cross


def body(
    chips,
    sigma_root,
    linv_one,
    panel_one,
    tiles_one,
    mask_one,
    linv_two,
    panel_two,
    tiles_two,
    mask_two,
    parent,
):
    leaf_id = lax.axis_index("leaf")
    width = sigma_root.shape[1]
    own_tiles = lax.dynamic_index_in_dim(tiles_one, leaf_id, 0, keepdims=False)
    selected_first = jnp.take(sigma_root, pattern_rows(own_tiles), axis=0)
    select_first = lax.psum(spread_tiles(selected_first, own_tiles), "row")
    masked_one = panel_one[0] * expand_mask(mask_one[0]).astype(jnp.bfloat16)
    masked_two = panel_two[0] * expand_mask(mask_two[0]).astype(jnp.bfloat16)
    whole_one, blocks_one = gather_block(masked_one, linv_one[0], chips, 0)
    sigma_first, cross_first = finish_block(select_first, whole_one, blocks_one, linv_one[0])
    rows_every = pattern_rows(tiles_two)
    count, block_rows = rows_every.shape
    owned = (parent == leaf_id).astype(jnp.float32)
    slots = jnp.take(sigma_first, rows_every.reshape(-1), axis=0).reshape(count, block_rows, width)
    slots = slots * owned[:, None, None]
    arrived = lax.all_to_all(slots, "leaf", split_axis=0, concat_axis=0, tiled=True)
    arrived, masked_two, linv_second = lax.optimization_barrier((arrived, masked_two, linv_two[0]))
    selected_second = jnp.sum(arrived, axis=0)
    tiles_second = lax.dynamic_index_in_dim(tiles_two, leaf_id, 0, keepdims=False)
    select_second = lax.psum(spread_tiles(selected_second, tiles_second), "row")
    whole_two, blocks_two = gather_block(masked_two, linv_second, chips, 1)
    sigma_second, cross_second = finish_block(select_second, whole_two, blocks_two, linv_second)
    return (sigma_first[None], cross_first[None], sigma_second[None], cross_second[None])


def solution(mesh):
    chips = mesh.shape["row"] // 2
    return jax.shard_map(
        functools.partial(body, chips),
        mesh=mesh,
        in_specs=(
            P(None, "row"),
            P("leaf", None, "row"),
            P("leaf", None, "row"),
            P(),
            P("leaf", None, "row"),
            P("leaf", None, "row"),
            P("leaf", None, "row"),
            P(),
            P("leaf", None, "row"),
            P(),
        ),
        out_specs=(
            P("leaf", None, "row"),
            P("leaf", None, "row"),
            P("leaf", None, "row"),
            P("leaf", None, "row"),
        ),
        check_vma=False,
    )
```

```python
import functools

import jax
import jax.numpy as jnp
from jax import lax
from jax.experimental import pallas as pl
from jax.experimental.pallas import tpu as pltpu
from jax.sharding import PartitionSpec as P

TILE = 128
MESH = pl.DeviceIdType.MESH
HIGH = lax.Precision.HIGH


def expand_mask(tile_mask):
    return jnp.repeat(jnp.repeat(tile_mask, TILE, axis=0), TILE, axis=1)


def greet(barrier, where):
    pl.semaphore_signal(barrier, inc=1, device_id=where, device_id_type=MESH)


def greet_line(barrier, chips, extra):
    row = lax.axis_index("row")
    z = lax.div(row, 2)
    greet(barrier, {"row": row + 1 - 2 * lax.rem(row, 2)})

    @pl.when(z > 0)
    def _():
        greet(barrier, {"row": row - 2})

    @pl.when(z < chips - 1)
    def _():
        greet(barrier, {"row": row + 2})

    @pl.when(jnp.logical_or(z == 0, z == chips - 1))
    def _():
        pl.semaphore_wait(barrier, 2 + extra)

    @pl.when(jnp.logical_and(z > 0, z < chips - 1))
    def _():
        pl.semaphore_wait(barrier, 3 + extra)


def landed(ref, semaphore):
    pltpu.make_async_copy(ref, ref, semaphore).wait()


def gather_kernel(chips, leaves, panel_ref, linv_ref, zero_ref, *rest):
    if leaves:
        slots, whole_panel, whole, arrivals = rest[:4]
        zrecv, zright, zleft, srecv, ssend, local, fill, lsend, lrecv = rest[4:]
    else:
        whole_panel, whole = rest[:2]
        zrecv, zright, zleft, srecv, ssend, local, fill = rest[2:]
    width = panel_ref.shape[1]
    step = 2 * width
    row = lax.axis_index("row")
    z = lax.div(row, 2)
    core = lax.rem(row, 2)
    right, left, sibling = row + 2, row - 2, row + 1 - 2 * core

    barrier = pltpu.get_barrier_semaphore()
    if leaves:
        leaf = lax.axis_index("leaf")
        for k in range(1, leaves):
            greet(barrier, {"leaf": lax.rem(leaf + k, leaves)})
    greet_line(barrier, chips, max(leaves - 1, 0))

    def place(s, c, piece):
        columns = pl.ds(pl.multiple_of((2 * s + c) * width, width), width)
        if piece == 0:
            return whole_panel.at[:, columns]
        return whole.at[pl.ds((s + piece - 1) * step, step), columns]

    def origin(s, piece):
        if piece == 0:
            return panel_ref
        return linv_ref.at[pl.ds((s + piece - 1) * step, step), :]

    def send(source, s, piece, sends, recvs, device):
        return pltpu.make_async_remote_copy(
            src_ref=source,
            dst_ref=place(s, core, piece),
            send_sem=sends.at[s, piece],
            recv_sem=recvs.at[s, piece],
            device_id={"row": device},
            device_id_type=MESH,
        )

    def pieces(s):
        return range(1 + chips - s)

    def copies(source, s, piece, go_right, go_left):
        out = []
        if go_right:
            out.append(send(source, s, piece, zright, zrecv, right))
        if go_left:
            out.append(send(source, s, piece, zleft, zrecv, left))
        out.append(send(source, s, piece, ssend, srecv, sibling))
        return out

    def own(s, piece):
        here = pltpu.make_async_copy(origin(s, piece), place(s, core, piece), local.at[piece])
        return copies(origin(s, piece), s, piece, s < chips - 1, s > 0) + [here]

    def zero_fill(s):
        return pltpu.make_async_copy(
            zero_ref.at[pl.ds(0, s * step), :],
            whole.at[pl.ds(0, s * step), pl.ds(s * step, step)],
            fill.at[s],
        )

    def across(k):
        peer = lax.rem(leaf + k, leaves)
        return pltpu.make_async_remote_copy(
            src_ref=slots.at[peer],
            dst_ref=arrivals.at[leaf],
            send_sem=lsend.at[k],
            recv_sem=lrecv.at[k],
            device_id={"leaf": peer},
            device_id_type=MESH,
        )

    for s in range(chips):
        @pl.when(z == s)
        def _(s=s):
            for piece in pieces(s):
                for copy in own(s, piece):
                    copy.start()

    if leaves:
        for k in range(1, leaves):
            across(k).start()
        keep = pltpu.make_async_copy(slots.at[leaf], arrivals.at[leaf], lsend.at[0])
        keep.start()
    for s in range(1, chips):
        zero_fill(s).start()

    def routes(hops):
        for s in range(chips):
            if s + hops < chips:
                yield s, s + hops, s + hops < chips - 1, False
            if s - hops >= 0:
                yield s, s - hops, False, s - hops > 0

    for hops in range(1, chips):
        for piece in range(chips + 1):
            for s, here, go_right, go_left in routes(hops):
                if piece in pieces(s):
                    @pl.when(z == here)
                    def _(s=s, piece=piece, go_right=go_right, go_left=go_left):
                        landed(place(s, core, piece), zrecv.at[s, piece])
                        for copy in copies(place(s, core, piece), s, piece, go_right, go_left):
                            copy.start()

    for s in range(chips):
        for piece in pieces(s):
            landed(place(s, 1 - core, piece), srecv.at[s, piece])

        @pl.when(z == s)
        def _(s=s):
            for piece in pieces(s):
                moves = own(s, piece)
                for copy in moves[:-1]:
                    copy.wait_send()
                moves[-1].wait()

    for hops in range(1, chips):
        for s, here, go_right, go_left in routes(hops):
            @pl.when(z == here)
            def _(s=s, go_right=go_right, go_left=go_left):
                for piece in pieces(s):
                    for copy in copies(place(s, core, piece), s, piece, go_right, go_left):
                        copy.wait_send()

    for s in range(1, chips):
        zero_fill(s).wait()
    if leaves:
        keep.wait()
        for k in range(1, leaves):
            across(k).wait_send()
            landed(arrivals.at[lax.rem(leaf + leaves - k, leaves)], lrecv.at[k])


def gather_block(panel, linv, chips, number, slots=None):
    order, width = linv.shape
    rows = panel.shape[0]
    step = 2 * width
    kind = linv.dtype
    any_space = pl.BlockSpec(memory_space=pl.ANY)
    shapes = [jax.ShapeDtypeStruct((rows, order), kind), jax.ShapeDtypeStruct((order, order), kind)]
    operands = [panel, linv, jnp.zeros((order - step, step), kind)]
    scratch = [pltpu.SemaphoreType.DMA((chips, chips + 1))] * 5
    scratch += [pltpu.SemaphoreType.DMA((chips + 1,)), pltpu.SemaphoreType.DMA((chips,))]
    leaves = 0
    if slots is not None:
        leaves = slots.shape[0]
        operands.append(slots)
        shapes.append(jax.ShapeDtypeStruct(slots.shape, slots.dtype))
        scratch += [pltpu.SemaphoreType.DMA((leaves,))] * 2
    moved = (rows * order + order * order) * 2
    return pl.pallas_call(
        functools.partial(gather_kernel, chips, leaves),
        out_shape=shapes,
        in_specs=[any_space] * len(operands),
        out_specs=[any_space] * len(shapes),
        scratch_shapes=scratch,
        compiler_params=pltpu.CompilerParams(collective_id=number, has_side_effects=True),
        cost_estimate=pl.CostEstimate(flops=0, bytes_accessed=moved * 20, transcendentals=0),
        name="gather_%d" % number,
    )(*operands)


CHUNKS = 4


def line_sum_kernel(chips, part_ref, out_ref, other, total, from_left, from_right, to_right, to_left, *sems):
    pair, fl, fr, sr, sl, back_send, back_recv = sems
    half = total.shape[0]
    size = half // CHUNKS
    row = lax.axis_index("row")
    z = lax.div(row, 2)
    core = lax.rem(row, 2)
    right, left, sibling = row + 2, row - 2, row + 1 - 2 * core
    greet_line(pltpu.get_barrier_semaphore(), chips, 0)

    def remote(source, target, sends, recvs, device):
        return pltpu.make_async_remote_copy(
            src_ref=source,
            dst_ref=target,
            send_sem=sends,
            recv_sem=recvs,
            device_id={"row": device},
            device_id_type=MESH,
        )

    mine = pl.ds(pl.multiple_of(core * half, half), half)
    theirs = pl.ds(pl.multiple_of((1 - core) * half, half), half)
    swap = remote(part_ref.at[theirs], other, pair.at[0], pair.at[1], sibling)
    swap.start()

    @pl.when(z == 0)
    def _():
        from_left[...] = jnp.zeros_like(from_left)

    @pl.when(z == chips - 1)
    def _():
        from_right[...] = jnp.zeros_like(from_right)

    swap.wait()
    total[...] = part_ref[mine] + other[...]

    def rightward(q):
        here = pl.ds(q * size, size)
        return remote(to_right.at[here], from_left.at[here], sr.at[q], fl.at[q], right)

    def leftward(q):
        here = pl.ds(q * size, size)
        return remote(to_left.at[here], from_right.at[here], sl.at[q], fr.at[q], left)

    def go_right():
        for q in range(CHUNKS):
            here = pl.ds(q * size, size)

            @pl.when(z > 0)
            def _(q=q, here=here):
                landed(from_left.at[here], fl.at[q])

            to_right[here] = total[here] + from_left[here]

            @pl.when(z < chips - 1)
            def _(q=q):
                rightward(q).start()

    def go_left():
        for q in range(CHUNKS):
            here = pl.ds(q * size, size)

            @pl.when(z < chips - 1)
            def _(q=q, here=here):
                landed(from_right.at[here], fr.at[q])

            to_left[here] = total[here] + from_right[here]

            @pl.when(z > 0)
            def _(q=q):
                leftward(q).start()

    @pl.when(z < chips // 2)
    def _():
        go_right()
        go_left()

    @pl.when(z >= chips // 2)
    def _():
        go_left()
        go_right()

    out_ref[mine] = to_right[...] + from_right[...]
    back = remote(out_ref.at[mine], out_ref.at[mine], back_send, back_recv, sibling)
    back.start()
    for q in range(CHUNKS):
        @pl.when(z < chips - 1)
        def _(q=q):
            rightward(q).wait_send()

        @pl.when(z > 0)
        def _(q=q):
            leftward(q).wait_send()

    back.wait_send()
    landed(out_ref.at[theirs], back_recv)


def line_sum(part, chips, number):
    rows, columns = part.shape
    half = rows // 2
    vmem = pl.BlockSpec(memory_space=pltpu.VMEM)
    chunked = pltpu.SemaphoreType.DMA((CHUNKS,))
    return pl.pallas_call(
        functools.partial(line_sum_kernel, chips),
        out_shape=jax.ShapeDtypeStruct(part.shape, part.dtype),
        in_specs=[vmem],
        out_specs=vmem,
        scratch_shapes=[pltpu.VMEM((half, columns), part.dtype)] * 6
        + [pltpu.SemaphoreType.DMA((2,))]
        + [chunked] * 4
        + [pltpu.SemaphoreType.DMA(())] * 2,
        compiler_params=pltpu.CompilerParams(
            collective_id=number, has_side_effects=True, vmem_limit_bytes=24 * 1024 * 1024
        ),
        name="line_sum",
    )(part)


def spread_tiles(selected, tile_list):
    width = selected.shape[1]
    per = width // TILE
    row = lax.axis_index("row")
    parts = []
    for a in range(tile_list.shape[0]):
        tile = tile_list[a]
        piece = jnp.zeros((selected.shape[0], TILE), selected.dtype)
        for k in range(per):
            hit = tile == row * per + k
            piece = piece + jnp.where(hit, selected[:, k * TILE:(k + 1) * TILE], 0.0)
        parts.append(piece)
    return jnp.concatenate(parts, axis=1)


def finish_block(select, whole_panel, whole, linv):
    width = linv.shape[1]
    row = lax.axis_index("row")
    across = (((0,), (0,)), ((), ()))
    upper = jnp.dot(whole_panel, whole, preferred_element_type=jnp.float32)
    gram = lax.dot_general(whole, linv, across, preferred_element_type=jnp.float32)
    own = lax.dynamic_slice_in_dim(upper, row * width, width, 1)
    cross = -jnp.dot(select, own, precision=HIGH)
    sigma = gram - lax.dot_general(upper, cross, across, precision=HIGH)
    return sigma, cross


def take_tiles(matrix, tile_list):
    return jnp.concatenate(
        [
            lax.dynamic_slice_in_dim(matrix, tile_list[a] * TILE, TILE, 0)
            for a in range(tile_list.shape[0])
        ],
        axis=0,
    )


def body(
    chips,
    sigma_root,
    linv_one,
    panel_one,
    tiles_one,
    mask_one,
    linv_two,
    panel_two,
    tiles_two,
    mask_two,
    parent,
):
    leaf_id = lax.axis_index("leaf")
    width = sigma_root.shape[1]
    own_tiles = lax.dynamic_index_in_dim(tiles_one, leaf_id, 0, keepdims=False)
    selected_first = take_tiles(sigma_root, own_tiles)
    select_first = lax.psum(spread_tiles(selected_first, own_tiles), "row")
    masked_one = panel_one[0] * expand_mask(mask_one[0]).astype(jnp.bfloat16)
    masked_two = panel_two[0] * expand_mask(mask_two[0]).astype(jnp.bfloat16)
    panel_first, whole_first = gather_block(masked_one, linv_one[0], chips, 0)
    sigma_first, cross_first = finish_block(select_first, panel_first, whole_first, linv_one[0])
    count, per_block = tiles_two.shape
    owned = (parent == leaf_id).astype(jnp.float32)
    slots = take_tiles(sigma_first, tiles_two.reshape(-1)).reshape(count, per_block * TILE, width)
    slots = slots * owned[:, None, None]
    panel_second, whole_second, arrived = gather_block(masked_two, linv_two[0], chips, 1, slots)
    tiles_second = lax.dynamic_index_in_dim(tiles_two, leaf_id, 0, keepdims=False)
    spread = spread_tiles(jnp.sum(arrived, axis=0), tiles_second)
    select_second = line_sum(spread, chips, 2)
    sigma_second, cross_second = finish_block(select_second, panel_second, whole_second, linv_two[0])
    return (sigma_first[None], cross_first[None], sigma_second[None], cross_second[None])


def solution(mesh):
    chips = mesh.shape["row"] // 2
    return jax.shard_map(
        functools.partial(body, chips),
        mesh=mesh,
        in_specs=(
            P(None, "row"),
            P("leaf", None, "row"),
            P("leaf", None, "row"),
            P(),
            P("leaf", None, "row"),
            P("leaf", None, "row"),
            P("leaf", None, "row"),
            P(),
            P("leaf", None, "row"),
            P(),
        ),
        out_specs=(
            P("leaf", None, "row"),
            P("leaf", None, "row"),
            P("leaf", None, "row"),
            P("leaf", None, "row"),
        ),
        check_vma=False,
    )
```

```python
import functools

import jax
import jax.numpy as jnp
from jax import lax
from jax.experimental import pallas as pl
from jax.experimental.pallas import tpu as pltpu
from jax.sharding import PartitionSpec as P

TILE = 128
MESH = pl.DeviceIdType.MESH
HIGH = lax.Precision.HIGH


def expand_mask(tile_mask):
    return jnp.repeat(jnp.repeat(tile_mask, TILE, axis=0), TILE, axis=1)


def greet(barrier, where):
    pl.semaphore_signal(barrier, inc=1, device_id=where, device_id_type=MESH)


def greet_line(barrier, chips, extra):
    row = lax.axis_index("row")
    z = lax.div(row, 2)
    greet(barrier, {"row": row + 1 - 2 * lax.rem(row, 2)})

    @pl.when(z > 0)
    def _():
        greet(barrier, {"row": row - 2})

    @pl.when(z < chips - 1)
    def _():
        greet(barrier, {"row": row + 2})

    @pl.when(jnp.logical_or(z == 0, z == chips - 1))
    def _():
        pl.semaphore_wait(barrier, 2 + extra)

    @pl.when(jnp.logical_and(z > 0, z < chips - 1))
    def _():
        pl.semaphore_wait(barrier, 3 + extra)


def landed(ref, semaphore):
    pltpu.make_async_copy(ref, ref, semaphore).wait()


def gather_kernel(chips, leaves, panel_ref, linv_ref, *rest):
    if leaves:
        slots, rest = rest[0], rest[1:]
    whole_panel, blocks, rest = rest[0], rest[1:chips + 1], rest[chips + 1:]
    if leaves:
        arrivals, lsend, lrecv = rest[0], rest[-2], rest[-1]
        rest = rest[1:-2]
    zrecv, zright, zleft, srecv, ssend, local = rest
    width = panel_ref.shape[1]
    step = 2 * width
    row = lax.axis_index("row")
    z = lax.div(row, 2)
    core = lax.rem(row, 2)
    right, left, sibling = row + 2, row - 2, row + 1 - 2 * core

    barrier = pltpu.get_barrier_semaphore()
    if leaves:
        leaf = lax.axis_index("leaf")
        for k in range(1, leaves):
            greet(barrier, {"leaf": lax.rem(leaf + k, leaves)})
    greet_line(barrier, chips, max(leaves - 1, 0))

    def place(s, c, piece):
        if piece == 0:
            return whole_panel.at[2 * s + c]
        return blocks[s].at[c, pl.ds((piece - 1) * step, step), :]

    def origin(s, piece):
        if piece == 0:
            return panel_ref
        return linv_ref.at[pl.ds((s + piece - 1) * step, step), :]

    def send(source, s, piece, sends, recvs, device):
        return pltpu.make_async_remote_copy(
            src_ref=source,
            dst_ref=place(s, core, piece),
            send_sem=sends.at[s, piece],
            recv_sem=recvs.at[s, piece],
            device_id={"row": device},
            device_id_type=MESH,
        )

    def pieces(s):
        return range(1 + chips - s)

    def copies(source, s, piece, go_right, go_left):
        out = []
        if go_right:
            out.append(send(source, s, piece, zright, zrecv, right))
        if go_left:
            out.append(send(source, s, piece, zleft, zrecv, left))
        out.append(send(source, s, piece, ssend, srecv, sibling))
        return out

    def own(s, piece):
        here = pltpu.make_async_copy(origin(s, piece), place(s, core, piece), local.at[piece])
        return copies(origin(s, piece), s, piece, s < chips - 1, s > 0) + [here]

    def across(k):
        peer = lax.rem(leaf + k, leaves)
        return pltpu.make_async_remote_copy(
            src_ref=slots.at[peer],
            dst_ref=arrivals.at[leaf],
            send_sem=lsend.at[k],
            recv_sem=lrecv.at[k],
            device_id={"leaf": peer},
            device_id_type=MESH,
        )

    for s in range(chips):
        @pl.when(z == s)
        def _(s=s):
            for piece in pieces(s):
                for copy in own(s, piece):
                    copy.start()

    if leaves:
        for k in range(1, leaves):
            across(k).start()
        keep = pltpu.make_async_copy(slots.at[leaf], arrivals.at[leaf], lsend.at[0])
        keep.start()

    def routes(hops):
        for s in range(chips):
            if s + hops < chips:
                yield s, s + hops, s + hops < chips - 1, False
            if s - hops >= 0:
                yield s, s - hops, False, s - hops > 0

    for hops in range(1, chips):
        for piece in range(chips + 1):
            for s, here, go_right, go_left in routes(hops):
                if piece in pieces(s):
                    @pl.when(z == here)
                    def _(s=s, piece=piece, go_right=go_right, go_left=go_left):
                        landed(place(s, core, piece), zrecv.at[s, piece])
                        for copy in copies(place(s, core, piece), s, piece, go_right, go_left):
                            copy.start()

    for s in range(chips):
        for piece in pieces(s):
            landed(place(s, 1 - core, piece), srecv.at[s, piece])

        @pl.when(z == s)
        def _(s=s):
            for piece in pieces(s):
                moves = own(s, piece)
                for copy in moves[:-1]:
                    copy.wait_send()
                moves[-1].wait()

    for hops in range(1, chips):
        for s, here, go_right, go_left in routes(hops):
            @pl.when(z == here)
            def _(s=s, go_right=go_right, go_left=go_left):
                for piece in pieces(s):
                    for copy in copies(place(s, core, piece), s, piece, go_right, go_left):
                        copy.wait_send()

    if leaves:
        keep.wait()
        for k in range(1, leaves):
            across(k).wait_send()
            landed(arrivals.at[lax.rem(leaf + leaves - k, leaves)], lrecv.at[k])


def gather_block(panel, linv, chips, number, slots=None):
    order, width = linv.shape
    rows = panel.shape[0]
    step = 2 * width
    kind = linv.dtype
    any_space = pl.BlockSpec(memory_space=pl.ANY)
    shapes = [jax.ShapeDtypeStruct((2 * chips, rows, width), kind)]
    shapes += [jax.ShapeDtypeStruct((2, order - s * step, width), kind) for s in range(chips)]
    operands = [panel, linv]
    scratch = [pltpu.SemaphoreType.DMA((chips, chips + 1))] * 5
    scratch += [pltpu.SemaphoreType.DMA((chips + 1,))]
    leaves = 0
    if slots is not None:
        leaves = slots.shape[0]
        operands.append(slots)
        shapes.append(jax.ShapeDtypeStruct(slots.shape, slots.dtype))
        scratch += [pltpu.SemaphoreType.DMA((leaves,))] * 2
    moved = (rows * order + order * order) * 2
    out = pl.pallas_call(
        functools.partial(gather_kernel, chips, leaves),
        out_shape=shapes,
        in_specs=[any_space] * len(operands),
        out_specs=[any_space] * len(shapes),
        scratch_shapes=scratch,
        compiler_params=pltpu.CompilerParams(collective_id=number, has_side_effects=True),
        cost_estimate=pl.CostEstimate(flops=0, bytes_accessed=moved * 20, transcendentals=0),
        name="gather_%d" % number,
    )(*operands)
    arrived = out[chips + 1] if leaves else None
    return out[0], out[1:chips + 1], arrived


CHUNKS = 4


def line_sum_kernel(chips, part_ref, out_ref, other, total, from_left, from_right, to_right, to_left, *sems):
    pair, fl, fr, sr, sl, back_send, back_recv = sems
    half = total.shape[0]
    size = half // CHUNKS
    row = lax.axis_index("row")
    z = lax.div(row, 2)
    core = lax.rem(row, 2)
    right, left, sibling = row + 2, row - 2, row + 1 - 2 * core
    greet_line(pltpu.get_barrier_semaphore(), chips, 0)

    def remote(source, target, sends, recvs, device):
        return pltpu.make_async_remote_copy(
            src_ref=source,
            dst_ref=target,
            send_sem=sends,
            recv_sem=recvs,
            device_id={"row": device},
            device_id_type=MESH,
        )

    mine = pl.ds(pl.multiple_of(core * half, half), half)
    theirs = pl.ds(pl.multiple_of((1 - core) * half, half), half)
    swap = remote(part_ref.at[theirs], other, pair.at[0], pair.at[1], sibling)
    swap.start()

    @pl.when(z == 0)
    def _():
        from_left[...] = jnp.zeros_like(from_left)

    @pl.when(z == chips - 1)
    def _():
        from_right[...] = jnp.zeros_like(from_right)

    swap.wait()
    total[...] = part_ref[mine] + other[...]

    def rightward(q):
        here = pl.ds(q * size, size)
        return remote(to_right.at[here], from_left.at[here], sr.at[q], fl.at[q], right)

    def leftward(q):
        here = pl.ds(q * size, size)
        return remote(to_left.at[here], from_right.at[here], sl.at[q], fr.at[q], left)

    def go_right():
        for q in range(CHUNKS):
            here = pl.ds(q * size, size)

            @pl.when(z > 0)
            def _(q=q, here=here):
                landed(from_left.at[here], fl.at[q])

            to_right[here] = total[here] + from_left[here]

            @pl.when(z < chips - 1)
            def _(q=q):
                rightward(q).start()

    def go_left():
        for q in range(CHUNKS):
            here = pl.ds(q * size, size)

            @pl.when(z < chips - 1)
            def _(q=q, here=here):
                landed(from_right.at[here], fr.at[q])

            to_left[here] = total[here] + from_right[here]

            @pl.when(z > 0)
            def _(q=q):
                leftward(q).start()

    @pl.when(z < chips // 2)
    def _():
        go_right()
        go_left()

    @pl.when(z >= chips // 2)
    def _():
        go_left()
        go_right()

    out_ref[mine] = to_right[...] + from_right[...]
    back = remote(out_ref.at[mine], out_ref.at[mine], back_send, back_recv, sibling)
    back.start()
    for q in range(CHUNKS):
        @pl.when(z < chips - 1)
        def _(q=q):
            rightward(q).wait_send()

        @pl.when(z > 0)
        def _(q=q):
            leftward(q).wait_send()

    back.wait_send()
    landed(out_ref.at[theirs], back_recv)


def line_sum(part, chips, number):
    rows, columns = part.shape
    half = rows // 2
    vmem = pl.BlockSpec(memory_space=pltpu.VMEM)
    chunked = pltpu.SemaphoreType.DMA((CHUNKS,))
    return pl.pallas_call(
        functools.partial(line_sum_kernel, chips),
        out_shape=jax.ShapeDtypeStruct(part.shape, part.dtype),
        in_specs=[vmem],
        out_specs=vmem,
        scratch_shapes=[pltpu.VMEM((half, columns), part.dtype)] * 6
        + [pltpu.SemaphoreType.DMA((2,))]
        + [chunked] * 4
        + [pltpu.SemaphoreType.DMA(())] * 2,
        compiler_params=pltpu.CompilerParams(
            collective_id=number, has_side_effects=True, vmem_limit_bytes=24 * 1024 * 1024
        ),
        name="line_sum",
    )(part)


def spread_tiles(selected, tile_list):
    width = selected.shape[1]
    per = width // TILE
    row = lax.axis_index("row")
    parts = []
    for a in range(tile_list.shape[0]):
        tile = tile_list[a]
        piece = jnp.zeros((selected.shape[0], TILE), selected.dtype)
        for k in range(per):
            hit = tile == row * per + k
            piece = piece + jnp.where(hit, selected[:, k * TILE:(k + 1) * TILE], 0.0)
        parts.append(piece)
    return jnp.concatenate(parts, axis=1)


def finish_block(select, panels, blocks, linv):
    width = linv.shape[1]
    row = lax.axis_index("row")
    across = (((0,), (0,)), ((), ()))
    whole_panel = jnp.concatenate([panels[r] for r in range(panels.shape[0])], axis=1)
    upper, gram = [], []
    for s, pair in enumerate(blocks):
        start = 2 * s * width
        for c in range(2):
            upper.append(
                jnp.dot(whole_panel[:, start:], pair[c], preferred_element_type=jnp.float32)
            )
            gram.append(
                lax.dot_general(pair[c], linv[start:], across, preferred_element_type=jnp.float32)
            )
    upper = jnp.concatenate(upper, axis=1)
    own = lax.dynamic_slice_in_dim(upper, row * width, width, 1)
    cross = -jnp.dot(select, own, precision=HIGH)
    sigma = jnp.concatenate(gram, axis=0) - lax.dot_general(upper, cross, across, precision=HIGH)
    return sigma, cross


def take_tiles(matrix, tile_list):
    return jnp.concatenate(
        [
            lax.dynamic_slice_in_dim(matrix, tile_list[a] * TILE, TILE, 0)
            for a in range(tile_list.shape[0])
        ],
        axis=0,
    )


def body(
    chips,
    sigma_root,
    linv_one,
    panel_one,
    tiles_one,
    mask_one,
    linv_two,
    panel_two,
    tiles_two,
    mask_two,
    parent,
):
    leaf_id = lax.axis_index("leaf")
    width = sigma_root.shape[1]
    own_tiles = lax.dynamic_index_in_dim(tiles_one, leaf_id, 0, keepdims=False)
    selected_first = take_tiles(sigma_root, own_tiles)
    select_first = lax.psum(spread_tiles(selected_first, own_tiles), "row")
    masked_one = panel_one[0] * expand_mask(mask_one[0]).astype(jnp.bfloat16)
    masked_two = panel_two[0] * expand_mask(mask_two[0]).astype(jnp.bfloat16)
    panel_first, whole_first, _ = gather_block(masked_one, linv_one[0], chips, 0)
    sigma_first, cross_first = finish_block(select_first, panel_first, whole_first, linv_one[0])
    count, per_block = tiles_two.shape
    owned = (parent == leaf_id).astype(jnp.float32)
    slots = take_tiles(sigma_first, tiles_two.reshape(-1)).reshape(count, per_block * TILE, width)
    slots = slots * owned[:, None, None]
    panel_second, whole_second, arrived = gather_block(masked_two, linv_two[0], chips, 1, slots)
    tiles_second = lax.dynamic_index_in_dim(tiles_two, leaf_id, 0, keepdims=False)
    spread = spread_tiles(jnp.sum(arrived, axis=0), tiles_second)
    select_second = line_sum(spread, chips, 2)
    sigma_second, cross_second = finish_block(select_second, panel_second, whole_second, linv_two[0])
    return (sigma_first[None], cross_first[None], sigma_second[None], cross_second[None])


def solution(mesh):
    chips = mesh.shape["row"] // 2
    return jax.shard_map(
        functools.partial(body, chips),
        mesh=mesh,
        in_specs=(
            P(None, "row"),
            P("leaf", None, "row"),
            P("leaf", None, "row"),
            P(),
            P("leaf", None, "row"),
            P("leaf", None, "row"),
            P("leaf", None, "row"),
            P(),
            P("leaf", None, "row"),
            P(),
        ),
        out_specs=(
            P("leaf", None, "row"),
            P("leaf", None, "row"),
            P("leaf", None, "row"),
            P("leaf", None, "row"),
        ),
        check_vma=False,
    )
```

```python
import functools

import jax
import jax.numpy as jnp
from jax import lax
from jax.experimental import pallas as pl
from jax.experimental.pallas import tpu as pltpu
from jax.sharding import PartitionSpec as P

TILE = 128
MESH = pl.DeviceIdType.MESH
HIGH = lax.Precision.HIGH


def expand_mask(tile_mask):
    return jnp.repeat(jnp.repeat(tile_mask, TILE, axis=0), TILE, axis=1)


def greet(barrier, where):
    pl.semaphore_signal(barrier, inc=1, device_id=where, device_id_type=MESH)


def greet_line(barrier, chips, extra):
    row = lax.axis_index("row")
    z = lax.div(row, 2)
    greet(barrier, {"row": row + 1 - 2 * lax.rem(row, 2)})

    @pl.when(z > 0)
    def _():
        greet(barrier, {"row": row - 2})

    @pl.when(z < chips - 1)
    def _():
        greet(barrier, {"row": row + 2})

    @pl.when(jnp.logical_or(z == 0, z == chips - 1))
    def _():
        pl.semaphore_wait(barrier, 2 + extra)

    @pl.when(jnp.logical_and(z > 0, z < chips - 1))
    def _():
        pl.semaphore_wait(barrier, 3 + extra)


def landed(ref, semaphore):
    pltpu.make_async_copy(ref, ref, semaphore).wait()


def gather_kernel(chips, leaves, panel_ref, linv_ref, *rest):
    if leaves:
        slots, rest = rest[0], rest[1:]
    whole_panel, blocks, rest = rest[0], rest[1:chips + 1], rest[chips + 1:]
    if leaves:
        arrivals, lsend, lrecv = rest[0], rest[-2], rest[-1]
        rest = rest[1:-2]
    zrecv, zright, zleft, srecv, ssend, local = rest
    width = panel_ref.shape[1]
    step = 2 * width
    row = lax.axis_index("row")
    z = lax.div(row, 2)
    core = lax.rem(row, 2)
    right, left, sibling = row + 2, row - 2, row + 1 - 2 * core

    barrier = pltpu.get_barrier_semaphore()
    if leaves:
        leaf = lax.axis_index("leaf")
        for k in range(1, leaves):
            greet(barrier, {"leaf": lax.rem(leaf + k, leaves)})
    greet_line(barrier, chips, max(leaves - 1, 0))

    def place(s, c, piece):
        if piece == 0:
            return whole_panel.at[:, pl.ds(pl.multiple_of((2 * s + c) * width, width), width)]
        return blocks[s].at[pl.ds((piece - 1) * step, step), pl.ds(pl.multiple_of(c * width, width), width)]

    def origin(s, piece):
        if piece == 0:
            return panel_ref
        return linv_ref.at[pl.ds((s + piece - 1) * step, step), :]

    def send(source, s, piece, sends, recvs, device):
        return pltpu.make_async_remote_copy(
            src_ref=source,
            dst_ref=place(s, core, piece),
            send_sem=sends.at[s, piece],
            recv_sem=recvs.at[s, piece],
            device_id={"row": device},
            device_id_type=MESH,
        )

    def pieces(s):
        return range(1 + chips - s)

    def copies(source, s, piece, go_right, go_left):
        out = []
        if go_right:
            out.append(send(source, s, piece, zright, zrecv, right))
        if go_left:
            out.append(send(source, s, piece, zleft, zrecv, left))
        out.append(send(source, s, piece, ssend, srecv, sibling))
        return out

    def own(s, piece):
        here = pltpu.make_async_copy(origin(s, piece), place(s, core, piece), local.at[piece])
        return copies(origin(s, piece), s, piece, s < chips - 1, s > 0) + [here]

    def across(k):
        peer = lax.rem(leaf + k, leaves)
        return pltpu.make_async_remote_copy(
            src_ref=slots.at[peer],
            dst_ref=arrivals.at[leaf],
            send_sem=lsend.at[k],
            recv_sem=lrecv.at[k],
            device_id={"leaf": peer},
            device_id_type=MESH,
        )

    for s in range(chips):
        @pl.when(z == s)
        def _(s=s):
            for piece in pieces(s):
                for copy in own(s, piece):
                    copy.start()

    if leaves:
        for k in range(1, leaves):
            across(k).start()
        keep = pltpu.make_async_copy(slots.at[leaf], arrivals.at[leaf], lsend.at[0])
        keep.start()

    def routes(hops):
        for s in range(chips):
            if s + hops < chips:
                yield s, s + hops, s + hops < chips - 1, False
            if s - hops >= 0:
                yield s, s - hops, False, s - hops > 0

    for hops in range(1, chips):
        for piece in range(chips + 1):
            for s, here, go_right, go_left in routes(hops):
                if piece in pieces(s):
                    @pl.when(z == here)
                    def _(s=s, piece=piece, go_right=go_right, go_left=go_left):
                        landed(place(s, core, piece), zrecv.at[s, piece])
                        for copy in copies(place(s, core, piece), s, piece, go_right, go_left):
                            copy.start()

    for s in range(chips):
        for piece in pieces(s):
            landed(place(s, 1 - core, piece), srecv.at[s, piece])

        @pl.when(z == s)
        def _(s=s):
            for piece in pieces(s):
                moves = own(s, piece)
                for copy in moves[:-1]:
                    copy.wait_send()
                moves[-1].wait()

    for hops in range(1, chips):
        for s, here, go_right, go_left in routes(hops):
            @pl.when(z == here)
            def _(s=s, go_right=go_right, go_left=go_left):
                for piece in pieces(s):
                    for copy in copies(place(s, core, piece), s, piece, go_right, go_left):
                        copy.wait_send()

    if leaves:
        keep.wait()
        for k in range(1, leaves):
            across(k).wait_send()
            landed(arrivals.at[lax.rem(leaf + leaves - k, leaves)], lrecv.at[k])


def gather_block(panel, linv, chips, number, slots=None):
    order, width = linv.shape
    rows = panel.shape[0]
    step = 2 * width
    kind = linv.dtype
    any_space = pl.BlockSpec(memory_space=pl.ANY)
    shapes = [jax.ShapeDtypeStruct((rows, order), kind)]
    shapes += [jax.ShapeDtypeStruct((order - s * step, step), kind) for s in range(chips)]
    operands = [panel, linv]
    scratch = [pltpu.SemaphoreType.DMA((chips, chips + 1))] * 5
    scratch += [pltpu.SemaphoreType.DMA((chips + 1,))]
    leaves = 0
    if slots is not None:
        leaves = slots.shape[0]
        operands.append(slots)
        shapes.append(jax.ShapeDtypeStruct(slots.shape, slots.dtype))
        scratch += [pltpu.SemaphoreType.DMA((leaves,))] * 2
    moved = (rows * order + order * order) * 2
    out = pl.pallas_call(
        functools.partial(gather_kernel, chips, leaves),
        out_shape=shapes,
        in_specs=[any_space] * len(operands),
        out_specs=[any_space] * len(shapes),
        scratch_shapes=scratch,
        compiler_params=pltpu.CompilerParams(collective_id=number, has_side_effects=True),
        cost_estimate=pl.CostEstimate(flops=0, bytes_accessed=moved * 20, transcendentals=0),
        name="gather_%d" % number,
    )(*operands)
    arrived = out[chips + 1] if leaves else None
    return out[0], out[1:chips + 1], arrived


CHUNKS = 4


def line_sum_kernel(chips, part_ref, out_ref, other, total, from_left, from_right, to_right, to_left, *sems):
    pair, fl, fr, sr, sl, back_send, back_recv = sems
    half = total.shape[0]
    size = half // CHUNKS
    row = lax.axis_index("row")
    z = lax.div(row, 2)
    core = lax.rem(row, 2)
    right, left, sibling = row + 2, row - 2, row + 1 - 2 * core
    greet_line(pltpu.get_barrier_semaphore(), chips, 0)

    def remote(source, target, sends, recvs, device):
        return pltpu.make_async_remote_copy(
            src_ref=source,
            dst_ref=target,
            send_sem=sends,
            recv_sem=recvs,
            device_id={"row": device},
            device_id_type=MESH,
        )

    mine = pl.ds(pl.multiple_of(core * half, half), half)
    theirs = pl.ds(pl.multiple_of((1 - core) * half, half), half)
    swap = remote(part_ref.at[theirs], other, pair.at[0], pair.at[1], sibling)
    swap.start()

    @pl.when(z == 0)
    def _():
        from_left[...] = jnp.zeros_like(from_left)

    @pl.when(z == chips - 1)
    def _():
        from_right[...] = jnp.zeros_like(from_right)

    swap.wait()
    total[...] = part_ref[mine] + other[...]

    def rightward(q):
        here = pl.ds(q * size, size)
        return remote(to_right.at[here], from_left.at[here], sr.at[q], fl.at[q], right)

    def leftward(q):
        here = pl.ds(q * size, size)
        return remote(to_left.at[here], from_right.at[here], sl.at[q], fr.at[q], left)

    def go_right():
        for q in range(CHUNKS):
            here = pl.ds(q * size, size)

            @pl.when(z > 0)
            def _(q=q, here=here):
                landed(from_left.at[here], fl.at[q])

            to_right[here] = total[here] + from_left[here]

            @pl.when(z < chips - 1)
            def _(q=q):
                rightward(q).start()

    def go_left():
        for q in range(CHUNKS):
            here = pl.ds(q * size, size)

            @pl.when(z < chips - 1)
            def _(q=q, here=here):
                landed(from_right.at[here], fr.at[q])

            to_left[here] = total[here] + from_right[here]

            @pl.when(z > 0)
            def _(q=q):
                leftward(q).start()

    @pl.when(z < chips // 2)
    def _():
        go_right()
        go_left()

    @pl.when(z >= chips // 2)
    def _():
        go_left()
        go_right()

    out_ref[mine] = to_right[...] + from_right[...]
    back = remote(out_ref.at[mine], out_ref.at[mine], back_send, back_recv, sibling)
    back.start()
    for q in range(CHUNKS):
        @pl.when(z < chips - 1)
        def _(q=q):
            rightward(q).wait_send()

        @pl.when(z > 0)
        def _(q=q):
            leftward(q).wait_send()

    back.wait_send()
    landed(out_ref.at[theirs], back_recv)


def line_sum(part, chips, number):
    rows, columns = part.shape
    half = rows // 2
    vmem = pl.BlockSpec(memory_space=pltpu.VMEM)
    chunked = pltpu.SemaphoreType.DMA((CHUNKS,))
    return pl.pallas_call(
        functools.partial(line_sum_kernel, chips),
        out_shape=jax.ShapeDtypeStruct(part.shape, part.dtype),
        in_specs=[vmem],
        out_specs=vmem,
        scratch_shapes=[pltpu.VMEM((half, columns), part.dtype)] * 6
        + [pltpu.SemaphoreType.DMA((2,))]
        + [chunked] * 4
        + [pltpu.SemaphoreType.DMA(())] * 2,
        compiler_params=pltpu.CompilerParams(
            collective_id=number, has_side_effects=True, vmem_limit_bytes=24 * 1024 * 1024
        ),
        name="line_sum",
    )(part)


def spread_tiles(selected, tile_list):
    width = selected.shape[1]
    per = width // TILE
    row = lax.axis_index("row")
    parts = []
    for a in range(tile_list.shape[0]):
        tile = tile_list[a]
        piece = jnp.zeros((selected.shape[0], TILE), selected.dtype)
        for k in range(per):
            hit = tile == row * per + k
            piece = piece + jnp.where(hit, selected[:, k * TILE:(k + 1) * TILE], 0.0)
        parts.append(piece)
    return jnp.concatenate(parts, axis=1)


def finish_block(select, whole_panel, blocks, linv):
    width = linv.shape[1]
    step = 2 * width
    row = lax.axis_index("row")
    upper = jnp.concatenate(
        [
            jnp.dot(whole_panel[:, s * step:], block, preferred_element_type=jnp.float32)
            for s, block in enumerate(blocks)
        ],
        axis=1,
    )
    own = lax.dynamic_slice_in_dim(upper, row * width, width, 1)
    cross = -jnp.dot(select, own, precision=HIGH)
    gram = jnp.concatenate(
        [
            lax.dot_general(
                block, linv[s * step:], (((0,), (0,)), ((), ())), preferred_element_type=jnp.float32
            )
            for s, block in enumerate(blocks)
        ],
        axis=0,
    )
    sigma = gram - lax.dot_general(upper, cross, (((0,), (0,)), ((), ())), precision=HIGH)
    return sigma, cross


def take_tiles(matrix, tile_list):
    return jnp.concatenate(
        [
            lax.dynamic_slice_in_dim(matrix, tile_list[a] * TILE, TILE, 0)
            for a in range(tile_list.shape[0])
        ],
        axis=0,
    )


def body(
    chips,
    sigma_root,
    linv_one,
    panel_one,
    tiles_one,
    mask_one,
    linv_two,
    panel_two,
    tiles_two,
    mask_two,
    parent,
):
    leaf_id = lax.axis_index("leaf")
    width = sigma_root.shape[1]
    own_tiles = lax.dynamic_index_in_dim(tiles_one, leaf_id, 0, keepdims=False)
    selected_first = take_tiles(sigma_root, own_tiles)
    select_first = lax.psum(spread_tiles(selected_first, own_tiles), "row")
    masked_one = panel_one[0] * expand_mask(mask_one[0]).astype(jnp.bfloat16)
    masked_two = panel_two[0] * expand_mask(mask_two[0]).astype(jnp.bfloat16)
    panel_first, whole_first, _ = gather_block(masked_one, linv_one[0], chips, 0)
    sigma_first, cross_first = finish_block(select_first, panel_first, whole_first, linv_one[0])
    count, per_block = tiles_two.shape
    owned = (parent == leaf_id).astype(jnp.float32)
    slots = take_tiles(sigma_first, tiles_two.reshape(-1)).reshape(count, per_block * TILE, width)
    slots = slots * owned[:, None, None]
    panel_second, whole_second, arrived = gather_block(masked_two, linv_two[0], chips, 1, slots)
    tiles_second = lax.dynamic_index_in_dim(tiles_two, leaf_id, 0, keepdims=False)
    spread = spread_tiles(jnp.sum(arrived, axis=0), tiles_second)
    select_second = line_sum(spread, chips, 2)
    sigma_second, cross_second = finish_block(select_second, panel_second, whole_second, linv_two[0])
    return (sigma_first[None], cross_first[None], sigma_second[None], cross_second[None])


def solution(mesh):
    chips = mesh.shape["row"] // 2
    return jax.shard_map(
        functools.partial(body, chips),
        mesh=mesh,
        in_specs=(
            P(None, "row"),
            P("leaf", None, "row"),
            P("leaf", None, "row"),
            P(),
            P("leaf", None, "row"),
            P("leaf", None, "row"),
            P("leaf", None, "row"),
            P(),
            P("leaf", None, "row"),
            P(),
        ),
        out_specs=(
            P("leaf", None, "row"),
            P("leaf", None, "row"),
            P("leaf", None, "row"),
            P("leaf", None, "row"),
        ),
        check_vma=False,
    )
```
